128 devices in a mesh: year: 8 (over x, core), date: 8 (over z_hi, y), pix: 2 (over z_lo).
Axes of the slice: x: 4, y: 4, z: 4 (z_hi: 2, z_lo: 2; z = z_hi * 2 + z_lo), core: 2. Of those that a mesh axis runs over, the one named last changes fastest.
Arguments:
- predicted_anomaly: bfloat16 [16, 8, 4, 83, 16384], P('year', 'date', None, None, 'pix'), may hold values from -6 to 6
- measured_anomaly: bfloat16 [16, 8, 4, 83, 16384], P('year', 'date', None, None, 'pix'), may hold values from -6 to 6
- filled_calendar: int32 [8], P('date'), may hold values from 1 to 4, 20 in all
Outputs:
- mean_error_field: float32 [8, 83, 2, 8192], P('date', None, 'pix', 'year')
- acc_map: float32 [83, 2, 8192], P(None, 'pix', ('year', 'date'))
- rmse_map: float32 [83, 2, 8192], P(None, 'pix', ('year', 'date'))
- scores: float32 [2, 83], replicated
The draws below stay inside these ranges and needn't reach their ends.
Inputs may be any that keep to these rules, and one draw needn't show every extreme that they name: `filled_calendar`: counts sum to 20, and some window uses all 4 slots.
All inputs are finite; a program needn't handle non-finite values. No bound on the sum of `filled_calendar` on one device may be relied on, other than what follows from the above.
Results may differ from the reference program's by a relative error of at most 0.0003.
Values sent between devices are 32-bit elements; how exact they have to be, the bound alone decides.
A program may use at most 128 MiB of HBM per device.

```python
import math
import jax
import jax.numpy as jnp
import numpy as np
from jax import lax

NUM_VARIABLES = 83
P_DEV = 8192
CALENDAR_SPOTS = 4
HINDCAST_SPAN = 16
SEASON_SPANS = 8
GRID_POINTS = 16384
N_PIX = 2


def levels(key, dims, shards, least, high):
    gain = 1.0
    for position, shards_of in shards:
        heights = jax.random.uniform(jax.random.fold_in(jax.random.fold_in(key, 6), position), (shards_of,), jnp.float32, least / len(shards), high / len(shards))
        gain = gain * jnp.repeat(jnp.exp(heights), dims[position] // shards_of).reshape((-1,) + (1,) * (len(dims) - 1 - position))
    return gain


def profile(count, total, limit, lean):
    weights = [(1 << 20) // math.isqrt(rank ** lean) + 1 for rank in range(2, count + 1)]
    rest, given = total - limit - (count - 1), [1] * (count - 1)
    while rest > 0:
        free = [i for i in range(count - 1) if given[i] < limit]
        pool, left = sum([weights[i] for i in free]), rest
        for i in free:
            addition = min(limit - given[i], max(1, left * weights[i] // pool), rest)
            given[i] = given[i] + addition
            rest = rest - addition
    return np.array([limit] + given)


def ragged(key, count, total, limit, slope):
    if count == 2:
        one = jax.random.randint(key, (), max(1, total - limit), min(limit, total - 1) + 1)
        return jnp.stack([one, total - one])
    tallies = jnp.asarray(profile(count, total, limit, slope), jnp.int32)
    pairs = (count - 1) // 2
    donor, receiver = tallies[1:1 + 2 * pairs:2], tallies[2:2 + 2 * pairs:2]
    margin = jnp.minimum(donor - 1, limit - receiver)
    shifted = jax.random.randint(jax.random.fold_in(key, 1), (pairs,), 0, 1 << 20) % (margin + 1)
    tallies = tallies.at[1:1 + 2 * pairs:2].set(donor - shifted).at[2:2 + 2 * pairs:2].set(receiver + shifted)
    return tallies[jax.random.permutation(jax.random.fold_in(key, 2), count)]


def gaussian(own_key, dims, scale, most, cuts=(), kind=jnp.bfloat16):
    values = scale * jax.random.normal(own_key, dims, jnp.float32)
    if cuts:
        values = values * levels(own_key, dims, cuts, -0.22, 0.18)
    return jnp.clip(values, -most, most).astype(kind)


def setup_inputs(seed: int = 0) -> dict:
    seeds = jax.random.split(jax.random.key(seed), 4)
    return {
        "predicted_anomaly": gaussian(seeds[0], (HINDCAST_SPAN, SEASON_SPANS, CALENDAR_SPOTS, NUM_VARIABLES, GRID_POINTS), 1.0, 6.0, ((0, 8), (1, 8), (4, 2))),
        "measured_anomaly": gaussian(seeds[1], (HINDCAST_SPAN, SEASON_SPANS, CALENDAR_SPOTS, NUM_VARIABLES, GRID_POINTS), 1.0, 6.0, ((0, 8), (1, 8), (4, 2))),
        "filled_calendar": ragged(seeds[2], SEASON_SPANS, 5 * SEASON_SPANS // 2, CALENDAR_SPOTS, 0).astype(jnp.int32),
    }


def reference(predicted_anomaly, measured_anomaly, filled_calendar):
    grid_extent = predicted_anomaly.shape[-1]
    variable_group = predicted_anomaly.shape[3]
    zero = jnp.zeros((variable_group, grid_extent), jnp.float32)
    s_fo, s_ff, s_oo, s_ee = (zero, zero, zero, zero)
    biases = []
    for season_number in range(SEASON_SPANS):
        predicted_season = predicted_anomaly[:, season_number].astype(jnp.float32)
        measured_season = measured_anomaly[:, season_number].astype(jnp.float32)
        valid = (jnp.arange(CALENDAR_SPOTS, dtype=jnp.int32) < filled_calendar[season_number]).astype(jnp.float32)[None, :, None, None]
        error_field = predicted_season - measured_season
        mean_error_field = lax.optimization_barrier(jnp.sum(valid * error_field, axis=(0, 1))) / (HINDCAST_SPAN * filled_calendar[season_number].astype(jnp.float32))
        biases.append(mean_error_field)
        corrected_anomaly = predicted_season - mean_error_field
        s_fo = s_fo + lax.optimization_barrier(jnp.sum(valid * corrected_anomaly * measured_season, axis=(0, 1)))
        s_ff = s_ff + lax.optimization_barrier(jnp.sum(valid * corrected_anomaly * corrected_anomaly, axis=(0, 1)))
        s_oo = s_oo + lax.optimization_barrier(jnp.sum(valid * measured_season * measured_season, axis=(0, 1)))
        spread = corrected_anomaly - measured_season
        s_ee = s_ee + lax.optimization_barrier(jnp.sum(valid * spread * spread, axis=(0, 1)))
    samples = HINDCAST_SPAN * jnp.sum(filled_calendar).astype(jnp.float32)
    acc = s_fo / jnp.sqrt(s_ff * s_oo + 1e-06)
    rmse = jnp.sqrt(s_ee / samples)
    rows = (jnp.arange(grid_extent, dtype=jnp.int32) % 181 - 90).astype(jnp.float32)
    lat_weight = jnp.cos(rows * (math.pi / 180.0))
    numer = jnp.stack([lax.optimization_barrier(jnp.sum(acc * lat_weight, axis=1)), lax.optimization_barrier(jnp.sum(rmse * lat_weight, axis=1))])
    scores = numer / jnp.sum(lat_weight)
    bias_out = jnp.stack(biases).reshape(SEASON_SPANS, variable_group, N_PIX, P_DEV)
    return (bias_out, acc.reshape(variable_group, N_PIX, P_DEV), rmse.reshape(variable_group, N_PIX, P_DEV), scores)
```

```python
import functools
import math

import jax
import jax.numpy as jnp
import numpy as np
from jax import lax
from jax.experimental import pallas as pl
from jax.experimental.pallas import tpu as pltpu
from jax.sharding import PartitionSpec as P

MESH = pl.DeviceIdType.MESH
F32 = jnp.float32
LANES = 128
TOTAL_COUNT = 20
E, T, OO, FF, EE = range(5)


def kernel(rows, years, dates, band, spans, weight_total, count_ref, f_hbm, o_hbm, bias_ref, acc_ref, rmse_ref, score_ref, *scratch):
    n_chunk = len(spans)
    per_chunk = 14
    bufs = [scratch[i * per_chunk:(i + 1) * per_chunk] for i in range(n_chunk)]
    (in_sem, send_sem, recv_sem, maps, mine, group_a, group_b, sa_sem, ra_sem, sb_sem, rb_sem) = scratch[n_chunk * per_chunk:]

    yr, dt, px = lax.axis_index("year"), lax.axis_index("date"), lax.axis_index("pix")
    x, c = yr // 2, yr % 2
    zh, y = dt // 4, dt % 4

    def device(dx=0, dc=0, dy=0, dz=0):
        return (((x + dx) % 4) * 2 + (c + dc) % 2, ((zh + dz) % 2) * 4 + (y + dy) % 4, px)

    loads = []
    for i, (first, high, _) in enumerate(spans):
        pair = []
        for which, (src, dst) in enumerate(((f_hbm, bufs[i][0]), (o_hbm, bufs[i][1]))):
            copy = pltpu.make_async_copy(
                src.at[:, 0, :, pl.ds(first, high), :], dst, in_sem.at[i, which])
            copy.start()
            pair.append(copy)
        loads.append(pair)

    barrier = pltpu.get_barrier_semaphore()
    for d in range(1, years):
        pl.semaphore_signal(barrier, inc=1, device_id=((yr + d) % years, dt, px), device_id_type=MESH)
    for d in range(1, 2 * dates):
        pl.semaphore_signal(
            barrier, inc=1, device_id=(yr, (dt + d // 2) % dates, (px + d % 2) % 2), device_id_type=MESH)

    maps[...] = jnp.zeros_like(maps)
    count = count_ref[0]
    weights = [(s < count).astype(F32) for s in range(4)]
    scale = 1.0 / (2 * years * count.astype(F32))

    sent = [[] for _ in range(n_chunk)]
    arriving = [{} for _ in range(n_chunk)]

    def send(i, name, src, dst, target):
        number = len(sent[i])
        copy = pltpu.make_async_remote_copy(
            src_ref=src, dst_ref=dst, send_sem=send_sem.at[i, number], recv_sem=recv_sem.at[i, number],
            device_id=target, device_id_type=MESH)
        copy.start()
        sent[i].append(copy)
        arriving[i].setdefault(name, []).append(copy)

    def arrive(i, name):
        for copy in arriving[i].pop(name):
            copy.wait_recv()

    def local_sums(i, n):
        fb, ob, w = bufs[i][0], bufs[i][1], bufs[i][2]
        height = spans[i][2]

        def step(km, carry):
            k, m = km // 2, km % 2
            base = ((((x + k) % 4) * 2 + (c + n) % 2) * 8 + ((zh + m) % 2) * 4) * LANES
            for j in range(4):
                lanes = pl.ds(pl.multiple_of(base + ((y + j) % 4) * LANES, LANES), LANES)
                totals = None
                for s in range(4):
                    vals = []
                    for year in range(2):
                        f = fb[year, s, :, lanes].astype(F32)[:height]
                        o = ob[year, s, :, lanes].astype(F32)[:height]
                        if s > 0:
                            f, o = f * weights[s], o * weights[s]
                        d = f - o
                        vals.append((f, o, f * f, o * o, d * d))
                    both = [a + b for a, b in zip(*vals)]
                    totals = both if totals is None else [a + b for a, b in zip(totals, both)]
                sf, so, ff, oo, ee = totals
                w[n, E, k, m, j] = sf - so
                w[n, T, k, m, j] = sf + so
                w[n, OO, k, m, j] = oo
                w[n, FF, k, m, j] = ff
                w[n, EE, k, m, j] = ee
            return carry

        lax.fori_loop(0, 8, step, 0)

    def stage0(i):
        w, dr = bufs[i][2], bufs[i][3]
        for copy in loads[i]:
            copy.wait()
        local_sums(i, 1)
        if i == 0:
            pl.semaphore_wait(barrier, years - 1 + 2 * dates - 1)
        send(i, "core", w.at[1], dr, device(dc=1))
        local_sums(i, 0)

    def stage1(i):
        (_, _, w, dr, x1, x2, y1e, y2e, ze, za, y1a, y2a, xq, late) = bufs[i]
        arrive(i, "core")

        def add(qk, carry):
            q, k = qk // 4, qk % 4
            w[0, q, k] = w[0, q, k] + dr[q, k]
            return carry

        lax.fori_loop(0, 20, add, 0)
        for h, way in enumerate((1, 3)):
            send(i, "x1", w.at[0, 0:2, 2, h], x1.at[h], device(dx=way))
        for h, way in enumerate((1, 3)):
            send(i, "y1e", w.at[0, 3:5, 1:4, h, 2], y1e.at[h], device(dy=way))
        send(i, "za", w.at[0, OO, :, 1], za, device(dz=1))

    def stage2(i):
        (_, _, w, dr, x1, x2, y1e, y2e, ze, za, y1a, y2a, xq, late) = bufs[i]
        arrive(i, "x1")
        w[0, 0:2, 1, 0] = w[0, 0:2, 1, 0] + x1[0]
        w[0, 0:2, 3, 1] = w[0, 0:2, 3, 1] + x1[1]
        send(i, "x2", w.at[0, 0:2, 1], x2.at[0], device(dx=1))
        send(i, "x2", w.at[0, 0:2, 3], x2.at[1], device(dx=3))
        arrive(i, "y1e")
        w[0, 3:5, 1:4, 0, 1] = w[0, 3:5, 1:4, 0, 1] + y1e[0]
        w[0, 3:5, 1:4, 1, 3] = w[0, 3:5, 1:4, 1, 3] + y1e[1]
        send(i, "y2e", w.at[0, 3:5, 1:4, :, 1], y2e.at[0], device(dy=1))
        send(i, "y2e", w.at[0, 3:5, 1:4, :, 3], y2e.at[1], device(dy=3))
        arrive(i, "za")
        w[0, OO, :, 0] = w[0, OO, :, 0] + za[...]
        for h, way in enumerate((1, 3)):
            send(i, "y1a", w.at[0, OO, 2 * h:2 * h + 2, 0, 2], y1a.at[h], device(dy=way))

    def stage3(i):
        (_, _, w, dr, x1, x2, y1e, y2e, ze, za, y1a, y2a, xq, late) = bufs[i]
        first, high, height = spans[i]
        arrive(i, "x2")
        for m in range(2):
            for j in range(4):
                e = w[0, E, 0, m, j] + x2[0, E, m, j] + x2[1, E, m, j]
                t = w[0, T, 0, m, j] + x2[0, T, m, j] + x2[1, T, m, j]
                b = e * scale
                lanes = pl.ds(pl.multiple_of((((zh + m) % 2) * 4 + (y + j) % 4) * LANES, LANES), LANES)
                bias_ref[pl.ds(first, high), lanes] = b[:high]
                w[0, FF, 0, m, j] = w[0, FF, 0, m, j] - b * t
                w[0, EE, 0, m, j] = w[0, EE, 0, m, j] - b * e
        for h, way in enumerate((1, 3)):
            send(i, "y1l", w.at[0, 3:5, 0, h, 2], late.at[0, h], device(dy=way))
        arrive(i, "y2e")
        for m in range(2):
            w[0, 3:5, 1:4, m, 0] = w[0, 3:5, 1:4, m, 0] + y2e[0, :, :, m] + y2e[1, :, :, m]
        send(i, "ze", w.at[0, 3:5, 1:4, 1, 0], ze, device(dz=1))
        arrive(i, "y1a")
        w[0, OO, 0:2, 0, 1] = w[0, OO, 0:2, 0, 1] + y1a[0]
        w[0, OO, 2:4, 0, 3] = w[0, OO, 2:4, 0, 3] + y1a[1]
        send(i, "y2a", w.at[0, OO, :, 0, 1], y2a.at[0], device(dy=1))
        send(i, "y2a", w.at[0, OO, :, 0, 3], y2a.at[1], device(dy=3))

    def stage4(i):
        (_, _, w, dr, x1, x2, y1e, y2e, ze, za, y1a, y2a, xq, late) = bufs[i]
        arrive(i, "ze")
        w[0, 3:5, 1:4, 0, 0] = w[0, 3:5, 1:4, 0, 0] + ze[...]
        arrive(i, "y2a")
        w[0, OO, :, 0, 0] = w[0, OO, :, 0, 0] + y2a[0] + y2a[1]
        for k in range(1, 4):
            send(i, "xq", w.at[0, 2:5, k, 0, 0], xq.at[k - 1], device(dx=k))
        arrive(i, "y1l")
        w[0, 3:5, 0, 0, 1] = w[0, 3:5, 0, 0, 1] + late[0, 0]
        w[0, 3:5, 0, 1, 3] = w[0, 3:5, 0, 1, 3] + late[0, 1]
        send(i, "y2l", w.at[0, 3:5, 0, :, 1], late.at[1], device(dy=1))
        send(i, "y2l", w.at[0, 3:5, 0, :, 3], late.at[2], device(dy=3))

    def stage5(i):
        w, late = bufs[i][2], bufs[i][13]
        arrive(i, "y2l")
        for m in range(2):
            w[0, 3:5, 0, m, 0] = w[0, 3:5, 0, m, 0] + late[1, :, m] + late[2, :, m]
        send(i, "zl", w.at[0, 3:5, 0, 1, 0], late.at[3, 0], device(dz=1))

    def stage6(i):
        w, xq, late = bufs[i][2], bufs[i][12], bufs[i][13]
        first, high, height = spans[i]
        arrive(i, "zl")
        arrive(i, "xq")
        oo, ff, ee = [w[0, q, 0, 0, 0] + xq[0, q - 2] + xq[1, q - 2] + xq[2, q - 2] for q in (OO, FF, EE)]
        ff = ff + late[3, 0, 0]
        ee = ee + late[3, 0, 1]
        fo = 0.5 * (ff + oo - ee)
        acc = fo / jnp.sqrt(ff * oo + 1e-06)
        rmse = jnp.sqrt(jnp.maximum(ee, 0.0) / (2.0 * years * TOTAL_COUNT))
        acc_ref[pl.ds(first, high), :] = acc[:high]
        rmse_ref[pl.ds(first, high), :] = rmse[:high]
        maps[0, pl.ds(first, height), :] = acc
        maps[1, pl.ds(first, height), :] = rmse

    stages = (stage0, stage1, stage2, stage3, stage4, stage5, stage6)
    for turn in range(n_chunk + len(stages) - 1):
        for s in reversed(range(len(stages))):
            if 0 <= turn - s < n_chunk:
                stages[s](turn - s)

    pixel = px * band + (yr * dates + dt) * LANES + lax.broadcasted_iota(jnp.int32, (8, LANES), 1)
    lat = jnp.cos((pixel % 181 - 90).astype(F32) * (math.pi / 180.0))
    sums = [
        lax.dot_general(lat, maps[which], (((1,), (1,)), ((), ())), precision=lax.Precision.HIGHEST,
                        preferred_element_type=F32)
        for which in range(2)
    ]
    is_acc = lax.broadcasted_iota(jnp.int32, sums[0].shape, 0) == 0
    mine[...] = jnp.zeros_like(mine)
    mine[:, 0:sums[0].shape[1]] = jnp.where(is_acc, sums[0], sums[1])

    def exchange(own, group, ssem, rsem, me, n, target):
        copies = []
        for d in range(1, n):
            copy = pltpu.make_async_remote_copy(
                src_ref=own, dst_ref=group.at[me], send_sem=ssem.at[d], recv_sem=rsem.at[me],
                device_id=target(d), device_id_type=MESH)
            copy.start()
            copies.append(copy)
        group[me] = own[...]
        for d in range(1, n):
            other = (me + d) % n
            pltpu.make_async_remote_copy(
                src_ref=own, dst_ref=group.at[other], send_sem=ssem.at[d], recv_sem=rsem.at[other],
                device_id=target(d), device_id_type=MESH).wait_recv()
        for copy in copies:
            copy.wait_send()
        total = group[0]
        for d in range(1, n):
            total = total + group[d]
        return total

    own_sum = exchange(mine.at[0:8], group_a, sa_sem, ra_sem, yr, years, lambda d: ((yr + d) % years, dt, px))
    mine[...] = own_sum
    place = dt * 2 + px

    def in_group_b(d):
        other = (place + d) % (2 * dates)
        return (yr, other // 2, other % 2)

    total = exchange(mine.at[0:8], group_b, sb_sem, rb_sem, place, 2 * dates, in_group_b)
    score_ref[...] = total[0:2, 0:rows] * (1.0 / weight_total)
    for i in range(n_chunk):
        for copy in sent[i]:
            copy.wait_send()


def solution(mesh):
    years, dates = mesh.shape["year"], mesh.shape["date"]

    def body(predicted_anomaly, measured_anomaly, filled_calendar):
        _, _, slots, rows, band = predicted_anomaly.shape
        grid = band * mesh.shape["pix"]
        weight_total = float(np.sum(np.cos((np.arange(grid) % 181 - 90) * (math.pi / 180.0))))
        spans = []
        for first in range(0, rows, 16):
            high = min(16, rows - first)
            spans.append((first, high, high))
        scratch = []
        for _, rows_in, h in spans:
            def vm(*shape):
                return pltpu.VMEM((*shape, h, LANES), F32)
            scratch += [
                pltpu.VMEM((2, slots, rows_in, band), jnp.bfloat16),
                pltpu.VMEM((2, slots, rows_in, band), jnp.bfloat16),
                vm(2, 5, 4, 2, 4),
                vm(5, 4, 2, 4),
                vm(2, 2, 4),
                vm(2, 2, 2, 4),
                vm(2, 2, 3),
                vm(2, 2, 3, 2),
                vm(2, 3),
                vm(4, 4),
                vm(2, 2),
                vm(2, 4),
                vm(3, 3),
                vm(4, 2, 2),
            ]
        n_chunk = len(spans)
        tall = -(-rows // 8) * 8
        scratch += [
            pltpu.SemaphoreType.DMA((n_chunk, 2)),
            pltpu.SemaphoreType.DMA((n_chunk, 23)),
            pltpu.SemaphoreType.DMA((n_chunk, 23)),
            pltpu.VMEM((2, tall, LANES), F32),
            pltpu.VMEM((8, LANES), F32),
            pltpu.VMEM((years, 8, LANES), F32),
            pltpu.VMEM((2 * dates, 8, LANES), F32),
            pltpu.SemaphoreType.DMA((years,)),
            pltpu.SemaphoreType.DMA((years,)),
            pltpu.SemaphoreType.DMA((2 * dates,)),
            pltpu.SemaphoreType.DMA((2 * dates,)),
        ]
        bias, acc, rmse, scores = pl.pallas_call(
            functools.partial(kernel, rows, years, dates, band, spans, weight_total),
            name="bias_and_maps",
            out_shape=(
                jax.ShapeDtypeStruct((rows, band // years), F32),
                jax.ShapeDtypeStruct((rows, LANES), F32),
                jax.ShapeDtypeStruct((rows, LANES), F32),
                jax.ShapeDtypeStruct((2, rows), F32),
            ),
            in_specs=[
                pl.BlockSpec(memory_space=pltpu.SMEM),
                pl.BlockSpec(memory_space=pl.ANY),
                pl.BlockSpec(memory_space=pl.ANY),
            ],
            out_specs=[pl.BlockSpec(memory_space=pltpu.VMEM)] * 4,
            scratch_shapes=scratch,
            compiler_params=pltpu.CompilerParams(
                collective_id=0, has_side_effects=True, vmem_limit_bytes=60 * 2**20),
        )(filled_calendar, predicted_anomaly, measured_anomaly)
        return bias[None, :, None, :], acc[:, None, :], rmse[:, None, :], scores

    return jax.shard_map(
        body,
        mesh=mesh,
        in_specs=(P("year", "date", None, None, "pix"), P("year", "date", None, None, "pix"), P("date")),
        out_specs=(
            P("date", None, "pix", "year"),
            P(None, "pix", ("year", "date")),
            P(None, "pix", ("year", "date")),
            P(),
        ),
        check_vma=False,
    )
```

```python
import functools
import math

import jax
import jax.numpy as jnp
import numpy as np
from jax import lax
from jax.experimental import pallas as pl
from jax.experimental.pallas import tpu as pltpu
from jax.sharding import PartitionSpec as P

MESH = pl.DeviceIdType.MESH
F32 = jnp.float32
LANES = 128
TOTAL_COUNT = 20
E, T, OO, FF, EE = range(5)


def kernel(rows, years, dates, band, spans, weight_total, count_ref, f_hbm, o_hbm, bias_ref, acc_ref, rmse_ref, score_ref, *scratch):
    n_chunk = len(spans)
    per_chunk = 14
    bufs = [scratch[i * per_chunk:(i + 1) * per_chunk] for i in range(n_chunk)]
    (in_sem, wide, send_sem, recv_sem, maps, mine, group_a, group_b, sa_sem, ra_sem, sb_sem, rb_sem) = scratch[n_chunk * per_chunk:]

    yr, dt, px = lax.axis_index("year"), lax.axis_index("date"), lax.axis_index("pix")
    x, c = yr // 2, yr % 2
    zh, y = dt // 4, dt % 4

    def device(dx=0, dc=0, dy=0, dz=0):
        return (((x + dx) % 4) * 2 + (c + dc) % 2, ((zh + dz) % 2) * 4 + (y + dy) % 4, px)

    slots = 4

    def load(i, which):
        first, high, _ = spans[i]
        src, dst = (f_hbm, o_hbm)[which], bufs[i][which]

        def start(channel, carry):
            pltpu.make_async_copy(
                src.at[:, 0, first + channel],
                dst.at[:, pl.ds(pl.multiple_of(channel * slots, slots), slots), :],
                in_sem.at[i, which]).start()
            return carry

        lax.fori_loop(0, high, start, 0)

    for i in range(n_chunk):
        load(i, 0)
        load(i, 1)

    def loaded(i):
        first, high, _ = spans[i]
        for which, src in enumerate((f_hbm, o_hbm)):
            part = src.at[:, 0, pl.ds(first, high)]
            pltpu.make_async_copy(part, part, in_sem.at[i, which]).wait()

    barrier = pltpu.get_barrier_semaphore()
    for d in range(1, years):
        pl.semaphore_signal(barrier, inc=1, device_id=((yr + d) % years, dt, px), device_id_type=MESH)
    for d in range(1, 2 * dates):
        pl.semaphore_signal(
            barrier, inc=1, device_id=(yr, (dt + d // 2) % dates, (px + d % 2) % 2), device_id_type=MESH)

    maps[...] = jnp.zeros_like(maps)
    count = count_ref[0]
    weights = [(s < count).astype(F32) for s in range(4)]
    scale = 1.0 / (2 * years * count.astype(F32))

    sent = [[] for _ in range(n_chunk)]
    arriving = [{} for _ in range(n_chunk)]

    def send(i, name, src, dst, target):
        number = len(sent[i])
        copy = pltpu.make_async_remote_copy(
            src_ref=src, dst_ref=dst, send_sem=send_sem.at[i, number], recv_sem=recv_sem.at[i, number],
            device_id=target, device_id_type=MESH)
        copy.start()
        sent[i].append(copy)
        arriving[i].setdefault(name, []).append(copy)

    def arrive(i, name):
        for copy in arriving[i].pop(name):
            copy.wait_recv()

    def local_sums(i, n):
        fb, ob, w = bufs[i][0], bufs[i][1], bufs[i][2]
        height = spans[i][2]
        deep = fb.shape[1]

        def step(km, carry):
            k, m = km // 2, km % 2
            base = ((((x + k) % 4) * 2 + (c + n) % 2) * 8 + ((zh + m) % 2) * 4) * LANES
            for j in range(4):
                lanes = pl.ds(pl.multiple_of(base + ((y + j) % 4) * LANES, LANES), LANES)
                for year in range(2):
                    wide[j, 0, year, 0:deep] = fb[year, :, lanes].astype(F32)
                    wide[j, 1, year, 0:deep] = ob[year, :, lanes].astype(F32)
                totals = None
                for s in range(slots):
                    vals = []
                    for year in range(2):
                        f = wide[j, 0, year, pl.ds(s, height, stride=slots), :]
                        o = wide[j, 1, year, pl.ds(s, height, stride=slots), :]
                        if s > 0:
                            f, o = f * weights[s], o * weights[s]
                        d = f - o
                        vals.append((f, o, f * f, o * o, d * d))
                    both = [a + b for a, b in zip(*vals)]
                    totals = both if totals is None else [a + b for a, b in zip(totals, both)]
                sf, so, ff, oo, ee = totals
                w[n, E, k, m, j] = sf - so
                w[n, T, k, m, j] = sf + so
                w[n, OO, k, m, j] = oo
                w[n, FF, k, m, j] = ff
                w[n, EE, k, m, j] = ee
            return carry

        lax.fori_loop(0, 8, step, 0)

    def stage0(i):
        w, dr = bufs[i][2], bufs[i][3]
        loaded(i)
        local_sums(i, 1)
        if i == 0:
            pl.semaphore_wait(barrier, years - 1 + 2 * dates - 1)
        send(i, "core", w.at[1], dr, device(dc=1))
        local_sums(i, 0)

    def stage1(i):
        (_, _, w, dr, x1, x2, y1e, y2e, ze, za, y1a, y2a, xq, late) = bufs[i]
        arrive(i, "core")

        def add(qk, carry):
            q, k = qk // 4, qk % 4
            w[0, q, k] = w[0, q, k] + dr[q, k]
            return carry

        lax.fori_loop(0, 20, add, 0)
        for h, way in enumerate((1, 3)):
            send(i, "x1", w.at[0, 0:2, 2, h], x1.at[h], device(dx=way))
        for h, way in enumerate((1, 3)):
            send(i, "y1e", w.at[0, 3:5, 1:4, h, 2], y1e.at[h], device(dy=way))
        send(i, "za", w.at[0, OO, :, 1], za, device(dz=1))

    def stage2(i):
        (_, _, w, dr, x1, x2, y1e, y2e, ze, za, y1a, y2a, xq, late) = bufs[i]
        arrive(i, "x1")
        w[0, 0:2, 1, 0] = w[0, 0:2, 1, 0] + x1[0]
        w[0, 0:2, 3, 1] = w[0, 0:2, 3, 1] + x1[1]
        send(i, "x2", w.at[0, 0:2, 1], x2.at[0], device(dx=1))
        send(i, "x2", w.at[0, 0:2, 3], x2.at[1], device(dx=3))
        arrive(i, "y1e")
        w[0, 3:5, 1:4, 0, 1] = w[0, 3:5, 1:4, 0, 1] + y1e[0]
        w[0, 3:5, 1:4, 1, 3] = w[0, 3:5, 1:4, 1, 3] + y1e[1]
        send(i, "y2e", w.at[0, 3:5, 1:4, :, 1], y2e.at[0], device(dy=1))
        send(i, "y2e", w.at[0, 3:5, 1:4, :, 3], y2e.at[1], device(dy=3))
        arrive(i, "za")
        w[0, OO, :, 0] = w[0, OO, :, 0] + za[...]
        for h, way in enumerate((1, 3)):
            send(i, "y1a", w.at[0, OO, 2 * h:2 * h + 2, 0, 2], y1a.at[h], device(dy=way))

    def stage3(i):
        (_, _, w, dr, x1, x2, y1e, y2e, ze, za, y1a, y2a, xq, late) = bufs[i]
        first, high, height = spans[i]
        arrive(i, "x2")
        for m in range(2):
            for j in range(4):
                e = w[0, E, 0, m, j] + x2[0, E, m, j] + x2[1, E, m, j]
                t = w[0, T, 0, m, j] + x2[0, T, m, j] + x2[1, T, m, j]
                b = e * scale
                lanes = pl.ds(pl.multiple_of((((zh + m) % 2) * 4 + (y + j) % 4) * LANES, LANES), LANES)
                bias_ref[pl.ds(first, high), lanes] = b[:high]
                w[0, FF, 0, m, j] = w[0, FF, 0, m, j] - b * t
                w[0, EE, 0, m, j] = w[0, EE, 0, m, j] - b * e
        for h, way in enumerate((1, 3)):
            send(i, "y1l", w.at[0, 3:5, 0, h, 2], late.at[0, h], device(dy=way))
        arrive(i, "y2e")
        for m in range(2):
            w[0, 3:5, 1:4, m, 0] = w[0, 3:5, 1:4, m, 0] + y2e[0, :, :, m] + y2e[1, :, :, m]
        send(i, "ze", w.at[0, 3:5, 1:4, 1, 0], ze, device(dz=1))
        arrive(i, "y1a")
        w[0, OO, 0:2, 0, 1] = w[0, OO, 0:2, 0, 1] + y1a[0]
        w[0, OO, 2:4, 0, 3] = w[0, OO, 2:4, 0, 3] + y1a[1]
        send(i, "y2a", w.at[0, OO, :, 0, 1], y2a.at[0], device(dy=1))
        send(i, "y2a", w.at[0, OO, :, 0, 3], y2a.at[1], device(dy=3))

    def stage4(i):
        (_, _, w, dr, x1, x2, y1e, y2e, ze, za, y1a, y2a, xq, late) = bufs[i]
        arrive(i, "ze")
        w[0, 3:5, 1:4, 0, 0] = w[0, 3:5, 1:4, 0, 0] + ze[...]
        arrive(i, "y2a")
        w[0, OO, :, 0, 0] = w[0, OO, :, 0, 0] + y2a[0] + y2a[1]
        for k in range(1, 4):
            send(i, "xq", w.at[0, 2:5, k, 0, 0], xq.at[k - 1], device(dx=k))
        arrive(i, "y1l")
        w[0, 3:5, 0, 0, 1] = w[0, 3:5, 0, 0, 1] + late[0, 0]
        w[0, 3:5, 0, 1, 3] = w[0, 3:5, 0, 1, 3] + late[0, 1]
        send(i, "y2l", w.at[0, 3:5, 0, :, 1], late.at[1], device(dy=1))
        send(i, "y2l", w.at[0, 3:5, 0, :, 3], late.at[2], device(dy=3))

    def stage5(i):
        w, late = bufs[i][2], bufs[i][13]
        arrive(i, "y2l")
        for m in range(2):
            w[0, 3:5, 0, m, 0] = w[0, 3:5, 0, m, 0] + late[1, :, m] + late[2, :, m]
        send(i, "zl", w.at[0, 3:5, 0, 1, 0], late.at[3, 0], device(dz=1))

    def stage6(i):
        w, xq, late = bufs[i][2], bufs[i][12], bufs[i][13]
        first, high, height = spans[i]
        arrive(i, "zl")
        arrive(i, "xq")
        oo, ff, ee = [w[0, q, 0, 0, 0] + xq[0, q - 2] + xq[1, q - 2] + xq[2, q - 2] for q in (OO, FF, EE)]
        ff = ff + late[3, 0, 0]
        ee = ee + late[3, 0, 1]
        fo = 0.5 * (ff + oo - ee)
        acc = fo / jnp.sqrt(ff * oo + 1e-06)
        rmse = jnp.sqrt(jnp.maximum(ee, 0.0) / (2.0 * years * TOTAL_COUNT))
        acc_ref[pl.ds(first, high), :] = acc[:high]
        rmse_ref[pl.ds(first, high), :] = rmse[:high]
        maps[0, pl.ds(first, height), :] = acc
        maps[1, pl.ds(first, height), :] = rmse

    stages = (stage0, stage1, stage2, stage3, stage4, stage5, stage6)
    for turn in range(n_chunk + len(stages) - 1):
        for s in (1, 0, 2, 3, 4, 5, 6):
            if 0 <= turn - s < n_chunk:
                stages[s](turn - s)

    pixel = px * band + (yr * dates + dt) * LANES + lax.broadcasted_iota(jnp.int32, (8, LANES), 1)
    lat = jnp.cos((pixel % 181 - 90).astype(F32) * (math.pi / 180.0))
    sums = [
        lax.dot_general(lat, maps[which], (((1,), (1,)), ((), ())), precision=lax.Precision.HIGHEST,
                        preferred_element_type=F32)
        for which in range(2)
    ]
    is_acc = lax.broadcasted_iota(jnp.int32, sums[0].shape, 0) == 0
    mine[...] = jnp.zeros_like(mine)
    mine[:, 0:sums[0].shape[1]] = jnp.where(is_acc, sums[0], sums[1])

    def exchange(own, group, ssem, rsem, me, n, target):
        copies = []
        for d in range(1, n):
            copy = pltpu.make_async_remote_copy(
                src_ref=own, dst_ref=group.at[me], send_sem=ssem.at[d], recv_sem=rsem.at[me],
                device_id=target(d), device_id_type=MESH)
            copy.start()
            copies.append(copy)
        group[me] = own[...]
        for d in range(1, n):
            other = (me + d) % n
            pltpu.make_async_remote_copy(
                src_ref=own, dst_ref=group.at[other], send_sem=ssem.at[d], recv_sem=rsem.at[other],
                device_id=target(d), device_id_type=MESH).wait_recv()
        for copy in copies:
            copy.wait_send()
        total = group[0]
        for d in range(1, n):
            total = total + group[d]
        return total

    own_sum = exchange(mine.at[0:8], group_a, sa_sem, ra_sem, yr, years, lambda d: ((yr + d) % years, dt, px))
    mine[...] = own_sum
    place = dt * 2 + px

    def in_group_b(d):
        other = (place + d) % (2 * dates)
        return (yr, other // 2, other % 2)

    total = exchange(mine.at[0:8], group_b, sb_sem, rb_sem, place, 2 * dates, in_group_b)
    score_ref[...] = total[0:2, 0:rows] * (1.0 / weight_total)
    for i in range(n_chunk):
        for copy in sent[i]:
            copy.wait_send()


def solution(mesh):
    years, dates = mesh.shape["year"], mesh.shape["date"]

    def body(predicted_anomaly, measured_anomaly, filled_calendar):
        _, _, slots, rows, band = predicted_anomaly.shape
        grid = band * mesh.shape["pix"]
        weight_total = float(np.sum(np.cos((np.arange(grid) % 181 - 90) * (math.pi / 180.0))))
        spans = []
        for first in range(0, rows, 16):
            high = min(16, rows - first)
            spans.append((first, high, high))
        scratch = []
        for _, rows_in, h in spans:
            def vm(*shape):
                return pltpu.VMEM((*shape, h, LANES), F32)
            scratch += [
                pltpu.VMEM((2, -(-slots * rows_in // 16) * 16, band), jnp.bfloat16),
                pltpu.VMEM((2, -(-slots * rows_in // 16) * 16, band), jnp.bfloat16),
                vm(2, 5, 4, 2, 4),
                vm(5, 4, 2, 4),
                vm(2, 2, 4),
                vm(2, 2, 2, 4),
                vm(2, 2, 3),
                vm(2, 2, 3, 2),
                vm(2, 3),
                vm(4, 4),
                vm(2, 2),
                vm(2, 4),
                vm(3, 3),
                vm(4, 2, 2),
            ]
        n_chunk = len(spans)
        tall = -(-rows // 8) * 8
        scratch += [
            pltpu.SemaphoreType.DMA((n_chunk, 2)),
            pltpu.VMEM((4, 2, 2, slots * 16, LANES), F32),
            pltpu.SemaphoreType.DMA((n_chunk, 23)),
            pltpu.SemaphoreType.DMA((n_chunk, 23)),
            pltpu.VMEM((2, tall, LANES), F32),
            pltpu.VMEM((8, LANES), F32),
            pltpu.VMEM((years, 8, LANES), F32),
            pltpu.VMEM((2 * dates, 8, LANES), F32),
            pltpu.SemaphoreType.DMA((years,)),
            pltpu.SemaphoreType.DMA((years,)),
            pltpu.SemaphoreType.DMA((2 * dates,)),
            pltpu.SemaphoreType.DMA((2 * dates,)),
        ]
        bias, acc, rmse, scores = pl.pallas_call(
            functools.partial(kernel, rows, years, dates, band, spans, weight_total),
            name="bias_and_maps",
            out_shape=(
                jax.ShapeDtypeStruct((rows, band // years), F32),
                jax.ShapeDtypeStruct((rows, LANES), F32),
                jax.ShapeDtypeStruct((rows, LANES), F32),
                jax.ShapeDtypeStruct((2, rows), F32),
            ),
            in_specs=[
                pl.BlockSpec(memory_space=pltpu.SMEM),
                pl.BlockSpec(memory_space=pl.ANY),
                pl.BlockSpec(memory_space=pl.ANY),
            ],
            out_specs=[pl.BlockSpec(memory_space=pltpu.VMEM)] * 4,
            scratch_shapes=scratch,
            compiler_params=pltpu.CompilerParams(
                collective_id=0, has_side_effects=True, vmem_limit_bytes=60 * 2**20),
        )(filled_calendar, jnp.transpose(predicted_anomaly, (0, 1, 3, 2, 4)), jnp.transpose(measured_anomaly, (0, 1, 3, 2, 4)))
        return bias[None, :, None, :], acc[:, None, :], rmse[:, None, :], scores

    return jax.shard_map(
        body,
        mesh=mesh,
        in_specs=(P("year", "date", None, None, "pix"), P("year", "date", None, None, "pix"), P("date")),
        out_specs=(
            P("date", None, "pix", "year"),
            P(None, "pix", ("year", "date")),
            P(None, "pix", ("year", "date")),
            P(),
        ),
        check_vma=False,
    )
```

```python
import functools
import math

import jax
import jax.numpy as jnp
import numpy as np
from jax import lax
from jax.experimental import pallas as pl
from jax.experimental.pallas import tpu as pltpu
from jax.sharding import PartitionSpec as P

MESH = pl.DeviceIdType.MESH
F32 = jnp.float32
LANES = 128
TOTAL_COUNT = 20
E, T, OO, FF, EE = range(5)


def kernel(rows, years, dates, band, spans, weight_total, count_ref, f_hbm, o_hbm, bias_ref, acc_ref, rmse_ref, score_ref, *scratch):
    n_chunk = len(spans)
    per_chunk = 14
    bufs = [scratch[i * per_chunk:(i + 1) * per_chunk] for i in range(n_chunk)]
    (in_sem, wide, lat_ref, send_sem, recv_sem, maps, mine, group_a, group_b, sa_sem, ra_sem, sb_sem, rb_sem) = scratch[n_chunk * per_chunk:]

    yr, dt, px = lax.axis_index("year"), lax.axis_index("date"), lax.axis_index("pix")
    x, c = yr // 2, yr % 2
    zh, y = dt // 4, dt % 4

    def device(dx=0, dc=0, dy=0, dz=0):
        return (((x + dx) % 4) * 2 + (c + dc) % 2, ((zh + dz) % 2) * 4 + (y + dy) % 4, px)

    barrier = pltpu.get_barrier_semaphore()
    for d in range(1, years):
        pl.semaphore_signal(barrier, inc=1, device_id=((yr + d) % years, dt, px), device_id_type=MESH)
    for d in range(1, 2 * dates):
        pl.semaphore_signal(
            barrier, inc=1, device_id=(yr, (dt + d // 2) % dates, (px + d % 2) % 2), device_id_type=MESH)

    slots = 4

    def load(i, which):
        first, high, _ = spans[i]
        src, dst = (f_hbm, o_hbm)[which], bufs[i][which]

        def start(channel, carry):
            pltpu.make_async_copy(
                src.at[:, 0, first + channel],
                dst.at[:, pl.ds(pl.multiple_of(channel * slots, slots), slots), :],
                in_sem.at[i, which]).start()
            return carry

        lax.fori_loop(0, high, start, 0)

    load(0, 0)
    load(0, 1)

    def loaded(i):
        first, high, _ = spans[i]
        for which, src in enumerate((f_hbm, o_hbm)):
            part = src.at[:, 0, pl.ds(first, high)]
            pltpu.make_async_copy(part, part, in_sem.at[i, which]).wait()

    for i in range(1, min(2, n_chunk)):
        load(i, 0)
        load(i, 1)
    maps[...] = jnp.zeros_like(maps)
    pixel = px * band + (yr * dates + dt) * LANES + lax.broadcasted_iota(jnp.int32, (8, LANES), 1)
    lat_ref[...] = jnp.cos((pixel % 181 - 90).astype(F32) * (math.pi / 180.0))
    count = count_ref[0]
    weights = [(s < count).astype(F32) for s in range(4)]
    scale = 1.0 / (2 * years * count.astype(F32))

    sent = [[] for _ in range(n_chunk)]
    arriving = [{} for _ in range(n_chunk)]

    def send(i, name, src, dst, target):
        number = len(sent[i])
        copy = pltpu.make_async_remote_copy(
            src_ref=src, dst_ref=dst, send_sem=send_sem.at[i, number], recv_sem=recv_sem.at[i, number],
            device_id=target, device_id_type=MESH)
        copy.start()
        sent[i].append(copy)
        arriving[i].setdefault(name, []).append(copy)

    def arrive(i, name):
        for copy in arriving[i].pop(name):
            copy.wait_recv()

    def local_sums(i, n):
        fb, ob, w = bufs[i][0], bufs[i][1], bufs[i][2]
        height = spans[i][2]
        deep = fb.shape[1]

        def step(km, carry):
            k, m = km // 2, km % 2
            base = ((((x + k) % 4) * 2 + (c + n) % 2) * 8 + ((zh + m) % 2) * 4) * LANES
            for j in range(4):
                lanes = pl.ds(pl.multiple_of(base + ((y + j) % 4) * LANES, LANES), LANES)
                for year in range(2):
                    wide[j, 0, year, 0:deep] = fb[year, :, lanes].astype(F32)
                    wide[j, 1, year, 0:deep] = ob[year, :, lanes].astype(F32)
                totals = None
                for s in range(slots):
                    vals = []
                    for year in range(2):
                        f = wide[j, 0, year, pl.ds(s, height, stride=slots), :]
                        o = wide[j, 1, year, pl.ds(s, height, stride=slots), :]
                        if s > 0:
                            f, o = f * weights[s], o * weights[s]
                        d = f - o
                        vals.append((f, o, f * f, o * o, d * d))
                    both = [a + b for a, b in zip(*vals)]
                    totals = both if totals is None else [a + b for a, b in zip(totals, both)]
                sf, so, ff, oo, ee = totals
                w[n, E, k, m, j] = sf - so
                w[n, T, k, m, j] = sf + so
                w[n, OO, k, m, j] = oo
                w[n, FF, k, m, j] = ff
                w[n, EE, k, m, j] = ee
            return carry

        lax.fori_loop(0, 8, step, 0)

    def stage0(i):
        w, dr = bufs[i][2], bufs[i][3]
        loaded(i)
        local_sums(i, 1)
        if i == 0:
            pl.semaphore_wait(barrier, years - 1 + 2 * dates - 1)
        send(i, "core", w.at[1], dr, device(dc=1))
        if i + 2 < n_chunk:
            load(i + 2, 0)
            load(i + 2, 1)

    def stage0b(i):
        local_sums(i, 0)

    def stage1(i):
        (_, _, w, dr, x1, x2, y1e, y2e, ze, za, y1a, y2a, xq, late) = bufs[i]
        arrive(i, "core")

        def add(qk, carry):
            q, k = qk // 4, qk % 4
            w[0, q, k] = w[0, q, k] + dr[q, k]
            return carry

        lax.fori_loop(0, 20, add, 0)
        for h, way in enumerate((1, 3)):
            send(i, "x1", w.at[0, 0:2, 2, h], x1.at[h], device(dx=way))
        for h, way in enumerate((1, 3)):
            send(i, "y1e", w.at[0, 3:5, 1:4, h, 2], y1e.at[h], device(dy=way))
        send(i, "za", w.at[0, OO, :, 1], za, device(dz=1))

    def stage2(i):
        (_, _, w, dr, x1, x2, y1e, y2e, ze, za, y1a, y2a, xq, late) = bufs[i]
        arrive(i, "x1")
        w[0, 0:2, 1, 0] = w[0, 0:2, 1, 0] + x1[0]
        w[0, 0:2, 3, 1] = w[0, 0:2, 3, 1] + x1[1]
        send(i, "x2", w.at[0, 0:2, 1], x2.at[0], device(dx=1))
        send(i, "x2", w.at[0, 0:2, 3], x2.at[1], device(dx=3))
        arrive(i, "y1e")
        w[0, 3:5, 1:4, 0, 1] = w[0, 3:5, 1:4, 0, 1] + y1e[0]
        w[0, 3:5, 1:4, 1, 3] = w[0, 3:5, 1:4, 1, 3] + y1e[1]
        send(i, "y2e", w.at[0, 3:5, 1:4, :, 1], y2e.at[0], device(dy=1))
        send(i, "y2e", w.at[0, 3:5, 1:4, :, 3], y2e.at[1], device(dy=3))
        arrive(i, "za")
        w[0, OO, :, 0] = w[0, OO, :, 0] + za[...]
        for h, way in enumerate((1, 3)):
            send(i, "y1a", w.at[0, OO, 2 * h:2 * h + 2, 0, 2], y1a.at[h], device(dy=way))

    def stage3(i):
        (_, _, w, dr, x1, x2, y1e, y2e, ze, za, y1a, y2a, xq, late) = bufs[i]
        first, high, height = spans[i]
        arrive(i, "x2")
        for m in range(2):
            for j in range(4):
                e = w[0, E, 0, m, j] + x2[0, E, m, j] + x2[1, E, m, j]
                t = w[0, T, 0, m, j] + x2[0, T, m, j] + x2[1, T, m, j]
                b = e * scale
                lanes = pl.ds(pl.multiple_of((((zh + m) % 2) * 4 + (y + j) % 4) * LANES, LANES), LANES)
                bias_ref[pl.ds(first, high), lanes] = b[:high]
                w[0, FF, 0, m, j] = w[0, FF, 0, m, j] - b * t
                w[0, EE, 0, m, j] = w[0, EE, 0, m, j] - b * e
        for r in range(1, 8):
            send(i, "late", w.at[0, 3:5, 0, r // 4, r % 4], late.at[r - 1], device(dy=r % 4, dz=r // 4))
        arrive(i, "y2e")
        for m in range(2):
            w[0, 3:5, 1:4, m, 0] = w[0, 3:5, 1:4, m, 0] + y2e[0, :, :, m] + y2e[1, :, :, m]
        send(i, "ze", w.at[0, 3:5, 1:4, 1, 0], ze, device(dz=1))
        arrive(i, "y1a")
        w[0, OO, 0:2, 0, 1] = w[0, OO, 0:2, 0, 1] + y1a[0]
        w[0, OO, 2:4, 0, 3] = w[0, OO, 2:4, 0, 3] + y1a[1]
        send(i, "y2a", w.at[0, OO, :, 0, 1], y2a.at[0], device(dy=1))
        send(i, "y2a", w.at[0, OO, :, 0, 3], y2a.at[1], device(dy=3))

    def stage4(i):
        (_, _, w, dr, x1, x2, y1e, y2e, ze, za, y1a, y2a, xq, late) = bufs[i]
        arrive(i, "ze")
        w[0, 3:5, 1:4, 0, 0] = w[0, 3:5, 1:4, 0, 0] + ze[...]
        arrive(i, "y2a")
        w[0, OO, :, 0, 0] = w[0, OO, :, 0, 0] + y2a[0] + y2a[1]
        for k in range(1, 4):
            send(i, "xq", w.at[0, 2:5, k, 0, 0], xq.at[k - 1], device(dx=k))

    def stage5(i):
        w, xq, late = bufs[i][2], bufs[i][12], bufs[i][13]
        first, high, height = spans[i]
        arrive(i, "late")
        arrive(i, "xq")
        oo, ff, ee = [w[0, q, 0, 0, 0] + xq[0, q - 2] + xq[1, q - 2] + xq[2, q - 2] for q in (OO, FF, EE)]
        for r in range(7):
            ff = ff + late[r, 0]
            ee = ee + late[r, 1]
        fo = 0.5 * (ff + oo - ee)
        acc = fo / jnp.sqrt(ff * oo + 1e-06)
        rmse = jnp.sqrt(jnp.maximum(ee, 0.0) / (2.0 * years * TOTAL_COUNT))
        acc_ref[pl.ds(first, high), :] = acc[:high]
        rmse_ref[pl.ds(first, high), :] = rmse[:high]
        maps[0, pl.ds(first, height), :] = acc
        maps[1, pl.ds(first, height), :] = rmse

    order = ((stage0, 0), (stage1, 1), (stage0b, 0), (stage2, 2), (stage3, 3), (stage4, 4), (stage5, 5))
    for turn in range(n_chunk + max(lag for _, lag in order)):
        for stage, lag in order:
            if 0 <= turn - lag < n_chunk:
                stage(turn - lag)

    lat = lat_ref[...]
    sums = [
        lax.dot_general(lat, maps[which], (((1,), (1,)), ((), ())), precision=lax.Precision.HIGHEST,
                        preferred_element_type=F32)
        for which in range(2)
    ]
    is_acc = lax.broadcasted_iota(jnp.int32, sums[0].shape, 0) == 0
    mine[...] = jnp.zeros_like(mine)
    mine[:, 0:sums[0].shape[1]] = jnp.where(is_acc, sums[0], sums[1])

    def exchange(own, group, ssem, rsem, me, n, target):
        copies = []
        for d in range(1, n):
            copy = pltpu.make_async_remote_copy(
                src_ref=own, dst_ref=group.at[me], send_sem=ssem.at[d], recv_sem=rsem.at[me],
                device_id=target(d), device_id_type=MESH)
            copy.start()
            copies.append(copy)
        group[me] = own[...]
        for d in range(1, n):
            other = (me + d) % n
            pltpu.make_async_remote_copy(
                src_ref=own, dst_ref=group.at[other], send_sem=ssem.at[d], recv_sem=rsem.at[other],
                device_id=target(d), device_id_type=MESH).wait_recv()
        for copy in copies:
            copy.wait_send()
        total = group[0]
        for d in range(1, n):
            total = total + group[d]
        return total

    own_sum = exchange(mine.at[0:8], group_a, sa_sem, ra_sem, yr, years, lambda d: ((yr + d) % years, dt, px))
    mine[...] = own_sum
    place = dt * 2 + px

    def in_group_b(d):
        other = (place + d) % (2 * dates)
        return (yr, other // 2, other % 2)

    total = exchange(mine.at[0:8], group_b, sb_sem, rb_sem, place, 2 * dates, in_group_b)
    score_ref[...] = total[0:2, 0:rows] * (1.0 / weight_total)
    for i in range(n_chunk):
        for copy in sent[i]:
            copy.wait_send()


def place(bias, acc, rmse, score, bias_out, acc_out, rmse_out, score_out, sem):
    copies = [
        pltpu.make_async_copy(bias, bias_out.at[:, 0, :], sem.at[0]),
        pltpu.make_async_copy(acc, acc_out.at[:, 0, :], sem.at[1]),
        pltpu.make_async_copy(rmse, rmse_out.at[:, 0, :], sem.at[2]),
        pltpu.make_async_copy(score, score_out, sem.at[3]),
    ]
    for copy in copies:
        copy.start()
    for copy in copies:
        copy.wait()


def solution(mesh):
    years, dates = mesh.shape["year"], mesh.shape["date"]

    def body(predicted_anomaly, measured_anomaly, filled_calendar):
        _, _, slots, rows, band = predicted_anomaly.shape
        grid = band * mesh.shape["pix"]
        weight_total = float(np.sum(np.cos((np.arange(grid) % 181 - 90) * (math.pi / 180.0))))
        spans, first = [], 0
        for high in (8, 16, 16, 16, 16, 11):
            spans.append((first, high, high))
            first += high
        assert first == rows
        scratch = []
        for _, rows_in, h in spans:
            def vm(*shape):
                return pltpu.VMEM((*shape, h, LANES), F32)
            scratch += [
                pltpu.VMEM((2, -(-slots * rows_in // 16) * 16, band), jnp.bfloat16),
                pltpu.VMEM((2, -(-slots * rows_in // 16) * 16, band), jnp.bfloat16),
                vm(2, 5, 4, 2, 4),
                vm(5, 4, 2, 4),
                vm(2, 2, 4),
                vm(2, 2, 2, 4),
                vm(2, 2, 3),
                vm(2, 2, 3, 2),
                vm(2, 3),
                vm(4, 4),
                vm(2, 2),
                vm(2, 4),
                vm(3, 3),
                vm(7, 2),
            ]
        n_chunk = len(spans)
        tall = -(-rows // 8) * 8
        scratch += [
            pltpu.SemaphoreType.DMA((n_chunk, 2)),
            pltpu.VMEM((4, 2, 2, slots * 16, LANES), F32),
            pltpu.VMEM((8, LANES), F32),
            pltpu.SemaphoreType.DMA((n_chunk, 25)),
            pltpu.SemaphoreType.DMA((n_chunk, 25)),
            pltpu.VMEM((2, tall, LANES), F32),
            pltpu.VMEM((8, LANES), F32),
            pltpu.VMEM((years, 8, LANES), F32),
            pltpu.VMEM((2 * dates, 8, LANES), F32),
            pltpu.SemaphoreType.DMA((years,)),
            pltpu.SemaphoreType.DMA((years,)),
            pltpu.SemaphoreType.DMA((2 * dates,)),
            pltpu.SemaphoreType.DMA((2 * dates,)),
        ]
        bias, acc, rmse, scores = pl.pallas_call(
            functools.partial(kernel, rows, years, dates, band, spans, weight_total),
            name="bias_and_maps",
            out_shape=(
                jax.ShapeDtypeStruct((rows, band // years), F32),
                jax.ShapeDtypeStruct((rows, LANES), F32),
                jax.ShapeDtypeStruct((rows, LANES), F32),
                jax.ShapeDtypeStruct((2, rows), F32),
            ),
            in_specs=[
                pl.BlockSpec(memory_space=pltpu.SMEM),
                pl.BlockSpec(memory_space=pl.ANY),
                pl.BlockSpec(memory_space=pl.ANY),
            ],
            out_specs=[pl.BlockSpec(memory_space=pltpu.VMEM)] * 4,
            scratch_shapes=scratch,
            compiler_params=pltpu.CompilerParams(
                collective_id=0, has_side_effects=True, vmem_limit_bytes=60 * 2**20),
        )(filled_calendar, jnp.transpose(predicted_anomaly, (0, 1, 3, 2, 4)), jnp.transpose(measured_anomaly, (0, 1, 3, 2, 4)))
        bias, acc, rmse, scores = pl.pallas_call(
            place,
            name="place_outputs",
            out_shape=(
                jax.ShapeDtypeStruct((rows, 1, band // years), F32),
                jax.ShapeDtypeStruct((rows, 1, LANES), F32),
                jax.ShapeDtypeStruct((rows, 1, LANES), F32),
                jax.ShapeDtypeStruct((2, rows), F32),
            ),
            in_specs=[pl.BlockSpec(memory_space=pltpu.VMEM)] * 4,
            out_specs=[pl.BlockSpec(memory_space=pl.ANY)] * 4,
            scratch_shapes=[pltpu.SemaphoreType.DMA((4,))],
        )(bias, acc, rmse, scores)
        return bias[None], acc, rmse, scores

    return jax.shard_map(
        body,
        mesh=mesh,
        in_specs=(P("year", "date", None, None, "pix"), P("year", "date", None, None, "pix"), P("date")),
        out_specs=(
            P("date", None, "pix", "year"),
            P(None, "pix", ("year", "date")),
            P(None, "pix", ("year", "date")),
            P(),
        ),
        check_vma=False,
    )
```

```python
import functools
import math

import jax
import jax.numpy as jnp
import numpy as np
from jax import lax
from jax.experimental import pallas as pl
from jax.experimental.pallas import tpu as pltpu
from jax.sharding import PartitionSpec as P

MESH = pl.DeviceIdType.MESH
F32 = jnp.float32
LANES = 128
TOTAL_COUNT = 20
E, T, OO, FF, EE = range(5)


def kernel(rows, years, dates, band, spans, weight_total, count_ref, f_hbm, o_hbm, bias_ref, acc_ref, rmse_ref, score_ref, *scratch):
    n_chunk = len(spans)
    per_chunk = 14
    bufs = [scratch[i * per_chunk:(i + 1) * per_chunk] for i in range(n_chunk)]
    (in_sem, wide, lat_ref, send_sem, recv_sem, maps, mine, group_a, group_b, sa_sem, ra_sem, sb_sem, rb_sem) = scratch[n_chunk * per_chunk:]

    yr, dt, px = lax.axis_index("year"), lax.axis_index("date"), lax.axis_index("pix")
    x, c = yr // 2, yr % 2
    zh, y = dt // 4, dt % 4

    def device(dx=0, dc=0, dy=0, dz=0):
        return (((x + dx) % 4) * 2 + (c + dc) % 2, ((zh + dz) % 2) * 4 + (y + dy) % 4, px)

    barrier = pltpu.get_barrier_semaphore()
    for d in range(1, years):
        pl.semaphore_signal(barrier, inc=1, device_id=((yr + d) % years, dt, px), device_id_type=MESH)
    for d in range(1, 2 * dates):
        pl.semaphore_signal(
            barrier, inc=1, device_id=(yr, (dt + d // 2) % dates, (px + d % 2) % 2), device_id_type=MESH)

    slots = 4

    def load(i, which):
        first, high, _ = spans[i]
        src, dst = (f_hbm, o_hbm)[which], bufs[i][which]

        def start(channel, carry):
            pltpu.make_async_copy(
                src.at[:, 0, first + channel],
                dst.at[:, pl.ds(pl.multiple_of(channel * slots, slots), slots), :],
                in_sem.at[i, which]).start()
            return carry

        lax.fori_loop(0, high, start, 0)

    load(0, 0)
    load(0, 1)

    def loaded(i):
        first, high, _ = spans[i]
        for which, src in enumerate((f_hbm, o_hbm)):
            part = src.at[:, 0, pl.ds(first, high)]
            pltpu.make_async_copy(part, part, in_sem.at[i, which]).wait()

    for i in range(1, min(2, n_chunk)):
        load(i, 0)
        load(i, 1)
    maps[...] = jnp.zeros_like(maps)
    pixel = px * band + (yr * dates + dt) * LANES + lax.broadcasted_iota(jnp.int32, (8, LANES), 1)
    lat_ref[...] = jnp.cos((pixel % 181 - 90).astype(F32) * (math.pi / 180.0))
    count = count_ref[0]
    weights = [(s < count).astype(F32) for s in range(4)]
    scale = 1.0 / (2 * years * count.astype(F32))

    sent = [[] for _ in range(n_chunk)]
    arriving = [{} for _ in range(n_chunk)]

    def send(i, name, src, dst, target):
        number = len(sent[i])
        copy = pltpu.make_async_remote_copy(
            src_ref=src, dst_ref=dst, send_sem=send_sem.at[i, number], recv_sem=recv_sem.at[i, number],
            device_id=target, device_id_type=MESH)
        copy.start()
        sent[i].append(copy)
        arriving[i].setdefault(name, []).append(copy)

    def arrive(i, name):
        for copy in arriving[i].pop(name):
            copy.wait_recv()

    def local_sums(i, n, m):
        fb, ob, w = bufs[i][0], bufs[i][1], bufs[i][2]
        height = spans[i][2]
        deep = fb.shape[1]

        def step(k, carry):
            base = ((((x + k) % 4) * 2 + (c + n) % 2) * 8 + ((zh + m) % 2) * 4) * LANES
            for j in range(4):
                lanes = pl.ds(pl.multiple_of(base + ((y + j) % 4) * LANES, LANES), LANES)
                for year in range(2):
                    wide[j, 0, year, 0:deep] = fb[year, :, lanes].astype(F32)
                    wide[j, 1, year, 0:deep] = ob[year, :, lanes].astype(F32)
                totals = None
                for s in range(slots):
                    vals = []
                    for year in range(2):
                        f = wide[j, 0, year, pl.ds(s, height, stride=slots), :]
                        o = wide[j, 1, year, pl.ds(s, height, stride=slots), :]
                        if s > 0:
                            f, o = f * weights[s], o * weights[s]
                        d = f - o
                        vals.append((f, o, f * f, o * o, d * d))
                    both = [a + b for a, b in zip(*vals)]
                    totals = both if totals is None else [a + b for a, b in zip(totals, both)]
                sf, so, ff, oo, ee = totals
                for q, value in ((E, sf - so), (T, sf + so), (OO, oo), (FF, ff), (EE, ee)):
                    w[n, q, k, m, j] = value if n else value + bufs[i][3][q, k, m, j]
            return carry

        lax.fori_loop(0, 4, step, 0)

    def stage0(i):
        w, dr = bufs[i][2], bufs[i][3]
        loaded(i)
        for m in (1, 0):
            local_sums(i, 1, m)
            if i == 0 and m == 1:
                pl.semaphore_wait(barrier, years - 1 + 2 * dates - 1)
            send(i, "core%d" % m, w.at[1, :, :, m], dr.at[:, :, m], device(dc=1))
        if i + 2 < n_chunk:
            load(i + 2, 0)
            load(i + 2, 1)


    def stage1(i):
        (_, _, w, dr, x1, x2, y1e, y2e, ze, za, y1a, y2a, xq, late) = bufs[i]
        for m, way in ((1, 3), (0, 1)):
            arrive(i, "core%d" % m)
            local_sums(i, 0, m)
            if m == 1:
                send(i, "za", w.at[0, OO, :, 1], za, device(dz=1))
            send(i, "x1", w.at[0, 0:2, 2, m], x1.at[m], device(dx=way))
            send(i, "y1e", w.at[0, 3:5, 1:4, m, 2], y1e.at[m], device(dy=way))

    def stage2(i):
        (_, _, w, dr, x1, x2, y1e, y2e, ze, za, y1a, y2a, xq, late) = bufs[i]
        arrive(i, "x1")
        w[0, 0:2, 1, 0] = w[0, 0:2, 1, 0] + x1[0]
        w[0, 0:2, 3, 1] = w[0, 0:2, 3, 1] + x1[1]
        send(i, "x2", w.at[0, 0:2, 1], x2.at[0], device(dx=1))
        send(i, "x2", w.at[0, 0:2, 3], x2.at[1], device(dx=3))
        arrive(i, "y1e")
        w[0, 3:5, 1:4, 0, 1] = w[0, 3:5, 1:4, 0, 1] + y1e[0]
        w[0, 3:5, 1:4, 1, 3] = w[0, 3:5, 1:4, 1, 3] + y1e[1]
        send(i, "y2e", w.at[0, 3:5, 1:4, :, 1], y2e.at[0], device(dy=1))
        send(i, "y2e", w.at[0, 3:5, 1:4, :, 3], y2e.at[1], device(dy=3))
        arrive(i, "za")
        w[0, OO, :, 0] = w[0, OO, :, 0] + za[...]
        for h, way in enumerate((1, 3)):
            send(i, "y1a", w.at[0, OO, 2 * h:2 * h + 2, 0, 2], y1a.at[h], device(dy=way))

    def stage3(i):
        (_, _, w, dr, x1, x2, y1e, y2e, ze, za, y1a, y2a, xq, late) = bufs[i]
        first, high, height = spans[i]
        arrive(i, "x2")
        for m in range(2):
            for j in range(4):
                e = w[0, E, 0, m, j] + x2[0, E, m, j] + x2[1, E, m, j]
                t = w[0, T, 0, m, j] + x2[0, T, m, j] + x2[1, T, m, j]
                b = e * scale
                lanes = pl.ds(pl.multiple_of((((zh + m) % 2) * 4 + (y + j) % 4) * LANES, LANES), LANES)
                bias_ref[pl.ds(first, high), lanes] = b[:high]
                w[0, FF, 0, m, j] = w[0, FF, 0, m, j] - b * t
                w[0, EE, 0, m, j] = w[0, EE, 0, m, j] - b * e
        for r in range(1, 8):
            send(i, "late", w.at[0, 3:5, 0, r // 4, r % 4], late.at[r - 1], device(dy=r % 4, dz=r // 4))
        arrive(i, "y2e")
        for m in range(2):
            w[0, 3:5, 1:4, m, 0] = w[0, 3:5, 1:4, m, 0] + y2e[0, :, :, m] + y2e[1, :, :, m]
        send(i, "ze", w.at[0, 3:5, 1:4, 1, 0], ze, device(dz=1))
        arrive(i, "y1a")
        w[0, OO, 0:2, 0, 1] = w[0, OO, 0:2, 0, 1] + y1a[0]
        w[0, OO, 2:4, 0, 3] = w[0, OO, 2:4, 0, 3] + y1a[1]
        send(i, "y2a", w.at[0, OO, :, 0, 1], y2a.at[0], device(dy=1))
        send(i, "y2a", w.at[0, OO, :, 0, 3], y2a.at[1], device(dy=3))

    def stage4(i):
        (_, _, w, dr, x1, x2, y1e, y2e, ze, za, y1a, y2a, xq, late) = bufs[i]
        arrive(i, "ze")
        w[0, 3:5, 1:4, 0, 0] = w[0, 3:5, 1:4, 0, 0] + ze[...]
        arrive(i, "y2a")
        w[0, OO, :, 0, 0] = w[0, OO, :, 0, 0] + y2a[0] + y2a[1]
        for k in range(1, 4):
            send(i, "xq", w.at[0, 2:5, k, 0, 0], xq.at[k - 1], device(dx=k))

    def stage5(i):
        w, xq, late = bufs[i][2], bufs[i][12], bufs[i][13]
        first, high, height = spans[i]
        arrive(i, "late")
        arrive(i, "xq")
        oo, ff, ee = [w[0, q, 0, 0, 0] + xq[0, q - 2] + xq[1, q - 2] + xq[2, q - 2] for q in (OO, FF, EE)]
        for r in range(7):
            ff = ff + late[r, 0]
            ee = ee + late[r, 1]
        fo = 0.5 * (ff + oo - ee)
        acc = fo / jnp.sqrt(ff * oo + 1e-06)
        rmse = jnp.sqrt(jnp.maximum(ee, 0.0) / (2.0 * years * TOTAL_COUNT))
        acc_ref[pl.ds(first, high), :] = acc[:high]
        rmse_ref[pl.ds(first, high), :] = rmse[:high]
        maps[0, pl.ds(first, height), :] = acc
        maps[1, pl.ds(first, height), :] = rmse

    order = ((stage0, 0), (stage1, 1), (stage2, 2), (stage3, 3), (stage4, 4), (stage5, 5))
    for turn in range(n_chunk + max(lag for _, lag in order)):
        for stage, lag in order:
            if 0 <= turn - lag < n_chunk:
                stage(turn - lag)

    lat = lat_ref[...]
    sums = [
        lax.dot_general(lat, maps[which], (((1,), (1,)), ((), ())), precision=lax.Precision.HIGHEST,
                        preferred_element_type=F32)
        for which in range(2)
    ]
    is_acc = lax.broadcasted_iota(jnp.int32, sums[0].shape, 0) == 0
    mine[...] = jnp.zeros_like(mine)
    mine[:, 0:sums[0].shape[1]] = jnp.where(is_acc, sums[0], sums[1])

    def exchange(own, group, ssem, rsem, me, n, target, hidden=()):
        copies = []
        for d in range(1, n):
            copy = pltpu.make_async_remote_copy(
                src_ref=own, dst_ref=group.at[me], send_sem=ssem.at[d], recv_sem=rsem.at[me],
                device_id=target(d), device_id_type=MESH)
            copy.start()
            copies.append(copy)
        group[me] = own[...]
        for copy in hidden:
            copy.wait_send()
        for d in range(1, n):
            other = (me + d) % n
            pltpu.make_async_remote_copy(
                src_ref=own, dst_ref=group.at[other], send_sem=ssem.at[d], recv_sem=rsem.at[other],
                device_id=target(d), device_id_type=MESH).wait_recv()
        for copy in copies:
            copy.wait_send()
        total = group[0]
        for d in range(1, n):
            total = total + group[d]
        return total

    own_sum = exchange(mine.at[0:8], group_a, sa_sem, ra_sem, yr, years, lambda d: ((yr + d) % years, dt, px),
                       [copy for copies in sent for copy in copies])
    mine[...] = own_sum
    place = dt * 2 + px

    def in_group_b(d):
        other = (place + d) % (2 * dates)
        return (yr, other // 2, other % 2)

    total = exchange(mine.at[0:8], group_b, sb_sem, rb_sem, place, 2 * dates, in_group_b)
    score_ref[...] = total[0:2, 0:rows] * (1.0 / weight_total)


def place(bias, acc, rmse, score, bias_out, acc_out, rmse_out, score_out, sem):
    copies = [
        pltpu.make_async_copy(bias, bias_out.at[:, 0, :], sem.at[0]),
        pltpu.make_async_copy(acc, acc_out.at[:, 0, :], sem.at[1]),
        pltpu.make_async_copy(rmse, rmse_out.at[:, 0, :], sem.at[2]),
        pltpu.make_async_copy(score, score_out, sem.at[3]),
    ]
    for copy in copies:
        copy.start()
    for copy in copies:
        copy.wait()


def solution(mesh):
    years, dates = mesh.shape["year"], mesh.shape["date"]

    def body(predicted_anomaly, measured_anomaly, filled_calendar):
        _, _, slots, rows, band = predicted_anomaly.shape
        grid = band * mesh.shape["pix"]
        weight_total = float(np.sum(np.cos((np.arange(grid) % 181 - 90) * (math.pi / 180.0))))
        spans, first = [], 0
        for high in (8, 16, 16, 16, 16, 11):
            spans.append((first, high, high))
            first += high
        assert first == rows
        scratch = []
        for _, rows_in, h in spans:
            def vm(*shape):
                return pltpu.VMEM((*shape, h, LANES), F32)
            scratch += [
                pltpu.VMEM((2, -(-slots * rows_in // 16) * 16, band), jnp.bfloat16),
                pltpu.VMEM((2, -(-slots * rows_in // 16) * 16, band), jnp.bfloat16),
                vm(2, 5, 4, 2, 4),
                vm(5, 4, 2, 4),
                vm(2, 2, 4),
                vm(2, 2, 2, 4),
                vm(2, 2, 3),
                vm(2, 2, 3, 2),
                vm(2, 3),
                vm(4, 4),
                vm(2, 2),
                vm(2, 4),
                vm(3, 3),
                vm(7, 2),
            ]
        n_chunk = len(spans)
        tall = -(-rows // 8) * 8
        scratch += [
            pltpu.SemaphoreType.DMA((n_chunk, 2)),
            pltpu.VMEM((4, 2, 2, -(-slots * max(h for _, _, h in spans) // 16) * 16, LANES), F32),
            pltpu.VMEM((8, LANES), F32),
            pltpu.SemaphoreType.DMA((n_chunk, 26)),
            pltpu.SemaphoreType.DMA((n_chunk, 26)),
            pltpu.VMEM((2, tall, LANES), F32),
            pltpu.VMEM((8, LANES), F32),
            pltpu.VMEM((years, 8, LANES), F32),
            pltpu.VMEM((2 * dates, 8, LANES), F32),
            pltpu.SemaphoreType.DMA((years,)),
            pltpu.SemaphoreType.DMA((years,)),
            pltpu.SemaphoreType.DMA((2 * dates,)),
            pltpu.SemaphoreType.DMA((2 * dates,)),
        ]
        bias, acc, rmse, scores = pl.pallas_call(
            functools.partial(kernel, rows, years, dates, band, spans, weight_total),
            name="bias_and_maps",
            out_shape=(
                jax.ShapeDtypeStruct((rows, band // years), F32),
                jax.ShapeDtypeStruct((rows, LANES), F32),
                jax.ShapeDtypeStruct((rows, LANES), F32),
                jax.ShapeDtypeStruct((2, rows), F32),
            ),
            in_specs=[
                pl.BlockSpec(memory_space=pltpu.SMEM),
                pl.BlockSpec(memory_space=pl.ANY),
                pl.BlockSpec(memory_space=pl.ANY),
            ],
            out_specs=[pl.BlockSpec(memory_space=pltpu.VMEM)] * 4,
            scratch_shapes=scratch,
            compiler_params=pltpu.CompilerParams(
                collective_id=0, has_side_effects=True, vmem_limit_bytes=60 * 2**20),
        )(filled_calendar, jnp.transpose(predicted_anomaly, (0, 1, 3, 2, 4)), jnp.transpose(measured_anomaly, (0, 1, 3, 2, 4)))
        bias, acc, rmse, scores = pl.pallas_call(
            place,
            name="place_outputs",
            out_shape=(
                jax.ShapeDtypeStruct((rows, 1, band // years), F32),
                jax.ShapeDtypeStruct((rows, 1, LANES), F32),
                jax.ShapeDtypeStruct((rows, 1, LANES), F32),
                jax.ShapeDtypeStruct((2, rows), F32),
            ),
            in_specs=[pl.BlockSpec(memory_space=pltpu.VMEM)] * 4,
            out_specs=[pl.BlockSpec(memory_space=pl.ANY)] * 4,
            scratch_shapes=[pltpu.SemaphoreType.DMA((4,))],
        )(bias, acc, rmse, scores)
        return bias[None], acc, rmse, scores

    return jax.shard_map(
        body,
        mesh=mesh,
        in_specs=(P("year", "date", None, None, "pix"), P("year", "date", None, None, "pix"), P("date")),
        out_specs=(
            P("date", None, "pix", "year"),
            P(None, "pix", ("year", "date")),
            P(None, "pix", ("year", "date")),
            P(),
        ),
        check_vma=False,
    )
```

```python
import functools
import math

import jax
import jax.numpy as jnp
import numpy as np
from jax import lax
from jax.experimental import pallas as pl
from jax.experimental.pallas import tpu as pltpu
from jax.sharding import PartitionSpec as P

MESH = pl.DeviceIdType.MESH
F32 = jnp.float32
LANES = 128
TOTAL_COUNT = 20
E, T, OO, FF, EE = range(5)


def kernel(rows, years, dates, band, spans, weight_total, count_ref, f_hbm, o_hbm, bias_ref, acc_ref, rmse_ref, score_ref, *scratch):
    n_chunk = len(spans)
    per_chunk = 14
    bufs = [scratch[i * per_chunk:(i + 1) * per_chunk] for i in range(n_chunk)]
    (in_sem, wide, lat_ref, send_sem, recv_sem, maps, mine, group_a, group_b, sa_sem, ra_sem, sb_sem, rb_sem) = scratch[n_chunk * per_chunk:]

    yr, dt, px = lax.axis_index("year"), lax.axis_index("date"), lax.axis_index("pix")
    x, c = yr // 2, yr % 2
    zh, y = dt // 4, dt % 4

    def device(dx=0, dc=0, dy=0, dz=0):
        return (((x + dx) % 4) * 2 + (c + dc) % 2, ((zh + dz) % 2) * 4 + (y + dy) % 4, px)

    barrier = pltpu.get_barrier_semaphore()
    for d in range(1, years):
        pl.semaphore_signal(barrier, inc=1, device_id=((yr + d) % years, dt, px), device_id_type=MESH)
    for d in range(1, 2 * dates):
        pl.semaphore_signal(
            barrier, inc=1, device_id=(yr, (dt + d // 2) % dates, (px + d % 2) % 2), device_id_type=MESH)

    slots = 4

    def load(i, which):
        first, high, _ = spans[i]
        src, dst = (f_hbm, o_hbm)[which], bufs[i][which]

        def start(channel, carry):
            pltpu.make_async_copy(
                src.at[:, 0, first + channel],
                dst.at[:, pl.ds(pl.multiple_of(channel * slots, slots), slots), :],
                in_sem.at[i, which]).start()
            return carry

        lax.fori_loop(0, high, start, 0)

    load(0, 0)
    load(0, 1)

    def loaded(i):
        first, high, _ = spans[i]
        for which, src in enumerate((f_hbm, o_hbm)):
            part = src.at[:, 0, pl.ds(first, high)]
            pltpu.make_async_copy(part, part, in_sem.at[i, which]).wait()

    for i in range(1, min(2, n_chunk)):
        load(i, 0)
        load(i, 1)
    maps[...] = jnp.zeros_like(maps)
    pixel = px * band + (yr * dates + dt) * LANES + lax.broadcasted_iota(jnp.int32, (8, LANES), 1)
    lat_ref[...] = jnp.cos((pixel % 181 - 90).astype(F32) * (math.pi / 180.0))
    count = count_ref[0]
    weights = [(s < count).astype(F32) for s in range(4)]
    scale = 1.0 / (2 * years * count.astype(F32))

    sent = [[] for _ in range(n_chunk)]
    arriving = [{} for _ in range(n_chunk)]

    def send(i, name, src, dst, target):
        number = len(sent[i])
        copy = pltpu.make_async_remote_copy(
            src_ref=src, dst_ref=dst, send_sem=send_sem.at[i, number], recv_sem=recv_sem.at[i, number],
            device_id=target, device_id_type=MESH)
        copy.start()
        sent[i].append(copy)
        arriving[i].setdefault(name, []).append(copy)

    def arrive(i, name):
        for copy in arriving[i].pop(name):
            copy.wait_recv()

    def local_sums(i, n, m):
        fb, ob, w = bufs[i][0], bufs[i][1], bufs[i][2]
        height = spans[i][2]
        deep = fb.shape[1]

        def step(k, carry):
            base = ((((x + k) % 4) * 2 + (c + n) % 2) * 8 + ((zh + m) % 2) * 4) * LANES
            for j in range(4):
                lanes = pl.ds(pl.multiple_of(base + ((y + j) % 4) * LANES, LANES), LANES)
                for year in range(2):
                    wide[j, 0, year, 0:deep] = fb[year, :, lanes].astype(F32)
                    wide[j, 1, year, 0:deep] = ob[year, :, lanes].astype(F32)
                totals = None
                for s in range(slots):
                    vals = []
                    for year in range(2):
                        f = wide[j, 0, year, pl.ds(s, height, stride=slots), :]
                        o = wide[j, 1, year, pl.ds(s, height, stride=slots), :]
                        if s > 0:
                            f, o = f * weights[s], o * weights[s]
                        d = f - o
                        vals.append((f, o, f * f, o * o, d * d))
                    both = [a + b for a, b in zip(*vals)]
                    totals = both if totals is None else [a + b for a, b in zip(totals, both)]
                sf, so, ff, oo, ee = totals
                for q, value in ((E, sf - so), (T, sf + so), (OO, oo), (FF, ff), (EE, ee)):
                    w[n, q, k, m, j] = value if n else value + bufs[i][3][q, k, m, j]
            return carry

        lax.fori_loop(0, 4, step, 0)

    def stage0(i):
        w, dr = bufs[i][2], bufs[i][3]
        loaded(i)
        for m in (1, 0):
            local_sums(i, 1, m)
            if i == 0 and m == 1:
                pl.semaphore_wait(barrier, years - 1 + 2 * dates - 1)
            send(i, "core%d" % m, w.at[1, :, :, m], dr.at[:, :, m], device(dc=1))
        if i + 2 < n_chunk:
            load(i + 2, 0)
            load(i + 2, 1)


    def stage1(i):
        (_, _, w, dr, x1, x2, y1e, y2e, ze, za, y1a, y2a, xq, late) = bufs[i]
        for m, way in ((1, 3), (0, 1)):
            arrive(i, "core%d" % m)
            local_sums(i, 0, m)
            if m == 1:
                send(i, "za", w.at[0, OO, :, 1], za, device(dz=1))
            send(i, "x1", w.at[0, 0:2, 2, m], x1.at[m], device(dx=way))
            send(i, "y1e", w.at[0, 3:5, 1:4, m, 2], y1e.at[m], device(dy=way))

    def stage2(i):
        (_, _, w, dr, x1, x2, y1e, y2e, ze, za, y1a, y2a, xq, late) = bufs[i]
        arrive(i, "x1")
        w[0, 0:2, 1, 0] = w[0, 0:2, 1, 0] + x1[0]
        w[0, 0:2, 3, 1] = w[0, 0:2, 3, 1] + x1[1]
        send(i, "x2", w.at[0, 0:2, 1], x2.at[0], device(dx=1))
        send(i, "x2", w.at[0, 0:2, 3], x2.at[1], device(dx=3))
        arrive(i, "y1e")
        w[0, 3:5, 1:4, 0, 1] = w[0, 3:5, 1:4, 0, 1] + y1e[0]
        w[0, 3:5, 1:4, 1, 3] = w[0, 3:5, 1:4, 1, 3] + y1e[1]
        send(i, "y2e", w.at[0, 3:5, 1:4, :, 1], y2e.at[0], device(dy=1))
        send(i, "y2e", w.at[0, 3:5, 1:4, :, 3], y2e.at[1], device(dy=3))
        arrive(i, "za")
        w[0, OO, :, 0] = w[0, OO, :, 0] + za[...]
        for h, way in enumerate((1, 3)):
            send(i, "y1a", w.at[0, OO, 2 * h:2 * h + 2, 0, 2], y1a.at[h], device(dy=way))

    def stage3(i):
        (_, _, w, dr, x1, x2, y1e, y2e, ze, za, y1a, y2a, xq, late) = bufs[i]
        first, high, height = spans[i]
        arrive(i, "y2e")
        for m in range(2):
            w[0, 3:5, 1:4, m, 0] = w[0, 3:5, 1:4, m, 0] + y2e[0, :, :, m] + y2e[1, :, :, m]
        send(i, "ze", w.at[0, 3:5, 1:4, 1, 0], ze, device(dz=1))
        arrive(i, "x2")
        for m in range(2):
            for j in range(4):
                e = w[0, E, 0, m, j] + x2[0, E, m, j] + x2[1, E, m, j]
                t = w[0, T, 0, m, j] + x2[0, T, m, j] + x2[1, T, m, j]
                b = e * scale
                lanes = pl.ds(pl.multiple_of((((zh + m) % 2) * 4 + (y + j) % 4) * LANES, LANES), LANES)
                bias_ref[pl.ds(first, high), lanes] = b[:high]
                w[0, FF, 0, m, j] = w[0, FF, 0, m, j] - b * t
                w[0, EE, 0, m, j] = w[0, EE, 0, m, j] - b * e
        for r in range(1, 8):
            send(i, "late", w.at[0, 3:5, 0, r // 4, r % 4], late.at[r - 1], device(dy=r % 4, dz=r // 4))
        arrive(i, "y1a")
        w[0, OO, 0:2, 0, 1] = w[0, OO, 0:2, 0, 1] + y1a[0]
        w[0, OO, 2:4, 0, 3] = w[0, OO, 2:4, 0, 3] + y1a[1]
        send(i, "y2a", w.at[0, OO, :, 0, 1], y2a.at[0], device(dy=1))
        send(i, "y2a", w.at[0, OO, :, 0, 3], y2a.at[1], device(dy=3))

    def stage4(i):
        (_, _, w, dr, x1, x2, y1e, y2e, ze, za, y1a, y2a, xq, late) = bufs[i]
        arrive(i, "ze")
        w[0, 3:5, 1:4, 0, 0] = w[0, 3:5, 1:4, 0, 0] + ze[...]
        arrive(i, "y2a")
        w[0, OO, :, 0, 0] = w[0, OO, :, 0, 0] + y2a[0] + y2a[1]
        for k in range(1, 4):
            send(i, "xq", w.at[0, 2:5, k, 0, 0], xq.at[k - 1], device(dx=k))

    def stage5(i):
        w, xq, late = bufs[i][2], bufs[i][12], bufs[i][13]
        first, high, height = spans[i]
        arrive(i, "late")
        arrive(i, "xq")
        oo, ff, ee = [w[0, q, 0, 0, 0] + xq[0, q - 2] + xq[1, q - 2] + xq[2, q - 2] for q in (OO, FF, EE)]
        for r in range(7):
            ff = ff + late[r, 0]
            ee = ee + late[r, 1]
        fo = 0.5 * (ff + oo - ee)
        acc = fo / jnp.sqrt(ff * oo + 1e-06)
        rmse = jnp.sqrt(jnp.maximum(ee, 0.0) / (2.0 * years * TOTAL_COUNT))
        acc_ref[pl.ds(first, high), :] = acc[:high]
        rmse_ref[pl.ds(first, high), :] = rmse[:high]
        maps[0, pl.ds(first, height), :] = acc
        maps[1, pl.ds(first, height), :] = rmse

    order = ((stage0, 0), (stage1, 1), (stage2, 2), (stage3, 3), (stage4, 4), (stage5, 5))
    for turn in range(n_chunk + max(lag for _, lag in order)):
        for stage, lag in order:
            if 0 <= turn - lag < n_chunk:
                stage(turn - lag)

    lat = lat_ref[...]
    sums = [
        lax.dot_general(lat, maps[which], (((1,), (1,)), ((), ())), precision=lax.Precision.HIGHEST,
                        preferred_element_type=F32)
        for which in range(2)
    ]
    is_acc = lax.broadcasted_iota(jnp.int32, sums[0].shape, 0) == 0
    mine[...] = jnp.zeros_like(mine)
    mine[:, 0:sums[0].shape[1]] = jnp.where(is_acc, sums[0], sums[1])

    def exchange(own, group, ssem, rsem, me, n, target, hidden=()):
        copies = []
        for d in range(1, n):
            copy = pltpu.make_async_remote_copy(
                src_ref=own, dst_ref=group.at[me], send_sem=ssem.at[d], recv_sem=rsem.at[me],
                device_id=target(d), device_id_type=MESH)
            copy.start()
            copies.append(copy)
        group[me] = own[...]
        for copy in hidden:
            copy.wait_send()
        for d in range(1, n):
            other = (me + d) % n
            pltpu.make_async_remote_copy(
                src_ref=own, dst_ref=group.at[other], send_sem=ssem.at[d], recv_sem=rsem.at[other],
                device_id=target(d), device_id_type=MESH).wait_recv()
        for copy in copies:
            copy.wait_send()
        total = group[0]
        for d in range(1, n):
            total = total + group[d]
        return total

    own_sum = exchange(mine.at[0:8], group_a, sa_sem, ra_sem, yr, years, lambda d: ((yr + d) % years, dt, px),
                       [copy for copies in sent for copy in copies])
    mine[...] = own_sum
    place = dt * 2 + px

    def in_group_b(d):
        other = (place + d) % (2 * dates)
        return (yr, other // 2, other % 2)

    total = exchange(mine.at[0:8], group_b, sb_sem, rb_sem, place, 2 * dates, in_group_b)
    score_ref[...] = total[0:2, 0:rows] * (1.0 / weight_total)


def place(bias, acc, rmse, score, bias_out, acc_out, rmse_out, score_out, sem):
    copies = [
        pltpu.make_async_copy(bias, bias_out.at[:, 0, :], sem.at[0]),
        pltpu.make_async_copy(acc, acc_out.at[:, 0, :], sem.at[1]),
        pltpu.make_async_copy(rmse, rmse_out.at[:, 0, :], sem.at[2]),
        pltpu.make_async_copy(score, score_out, sem.at[3]),
    ]
    for copy in copies:
        copy.start()
    for copy in copies:
        copy.wait()


def solution(mesh):
    years, dates = mesh.shape["year"], mesh.shape["date"]

    def body(predicted_anomaly, measured_anomaly, filled_calendar):
        _, _, slots, rows, band = predicted_anomaly.shape
        grid = band * mesh.shape["pix"]
        weight_total = float(np.sum(np.cos((np.arange(grid) % 181 - 90) * (math.pi / 180.0))))
        spans, first = [], 0
        for high in (8, 16, 16, 16, 16, 11):
            spans.append((first, high, high))
            first += high
        assert first == rows
        scratch = []
        for _, rows_in, h in spans:
            def vm(*shape):
                return pltpu.VMEM((*shape, h, LANES), F32)
            scratch += [
                pltpu.VMEM((2, -(-slots * rows_in // 16) * 16, band), jnp.bfloat16),
                pltpu.VMEM((2, -(-slots * rows_in // 16) * 16, band), jnp.bfloat16),
                vm(2, 5, 4, 2, 4),
                vm(5, 4, 2, 4),
                vm(2, 2, 4),
                vm(2, 2, 2, 4),
                vm(2, 2, 3),
                vm(2, 2, 3, 2),
                vm(2, 3),
                vm(4, 4),
                vm(2, 2),
                vm(2, 4),
                vm(3, 3),
                vm(7, 2),
            ]
        n_chunk = len(spans)
        tall = -(-rows // 8) * 8
        scratch += [
            pltpu.SemaphoreType.DMA((n_chunk, 2)),
            pltpu.VMEM((4, 2, 2, -(-slots * max(h for _, _, h in spans) // 16) * 16, LANES), F32),
            pltpu.VMEM((8, LANES), F32),
            pltpu.SemaphoreType.DMA((n_chunk, 26)),
            pltpu.SemaphoreType.DMA((n_chunk, 26)),
            pltpu.VMEM((2, tall, LANES), F32),
            pltpu.VMEM((8, LANES), F32),
            pltpu.VMEM((years, 8, LANES), F32),
            pltpu.VMEM((2 * dates, 8, LANES), F32),
            pltpu.SemaphoreType.DMA((years,)),
            pltpu.SemaphoreType.DMA((years,)),
            pltpu.SemaphoreType.DMA((2 * dates,)),
            pltpu.SemaphoreType.DMA((2 * dates,)),
        ]
        bias, acc, rmse, scores = pl.pallas_call(
            functools.partial(kernel, rows, years, dates, band, spans, weight_total),
            name="bias_and_maps",
            out_shape=(
                jax.ShapeDtypeStruct((rows, band // years), F32),
                jax.ShapeDtypeStruct((rows, LANES), F32),
                jax.ShapeDtypeStruct((rows, LANES), F32),
                jax.ShapeDtypeStruct((2, rows), F32),
            ),
            in_specs=[
                pl.BlockSpec(memory_space=pltpu.SMEM),
                pl.BlockSpec(memory_space=pl.ANY),
                pl.BlockSpec(memory_space=pl.ANY),
            ],
            out_specs=[pl.BlockSpec(memory_space=pltpu.VMEM)] * 4,
            scratch_shapes=scratch,
            compiler_params=pltpu.CompilerParams(
                collective_id=0, has_side_effects=True, vmem_limit_bytes=60 * 2**20),
        )(filled_calendar, jnp.transpose(predicted_anomaly, (0, 1, 3, 2, 4)), jnp.transpose(measured_anomaly, (0, 1, 3, 2, 4)))
        bias, acc, rmse, scores = pl.pallas_call(
            place,
            name="place_outputs",
            out_shape=(
                jax.ShapeDtypeStruct((rows, 1, band // years), F32),
                jax.ShapeDtypeStruct((rows, 1, LANES), F32),
                jax.ShapeDtypeStruct((rows, 1, LANES), F32),
                jax.ShapeDtypeStruct((2, rows), F32),
            ),
            in_specs=[pl.BlockSpec(memory_space=pltpu.VMEM)] * 4,
            out_specs=[pl.BlockSpec(memory_space=pl.ANY)] * 4,
            scratch_shapes=[pltpu.SemaphoreType.DMA((4,))],
        )(bias, acc, rmse, scores)
        return bias[None], acc, rmse, scores

    return jax.shard_map(
        body,
        mesh=mesh,
        in_specs=(P("year", "date", None, None, "pix"), P("year", "date", None, None, "pix"), P("date")),
        out_specs=(
            P("date", None, "pix", "year"),
            P(None, "pix", ("year", "date")),
            P(None, "pix", ("year", "date")),
            P(),
        ),
        check_vma=False,
    )
```
